32 devices in a mesh: groups: 2 (over y), train: 4 (over z), test: 4 (over x, core).
Axes of the slice: x: 2, y: 2, z: 4, core: 2. Of those that a mesh axis runs over, the one named last changes fastest.
Arguments:
- train_feat: bfloat16 [8192, 4096], P(('groups', 'train'), 'test'), parts along dimension 0, may hold values from -6 to 6
- test_feat: bfloat16 [2048, 4096], P(('groups', 'test'), 'train'), parts along dimension 0, may hold values from -6 to 6
- inverse_kernel: bfloat16 [4096, 4096], P('train'), may hold values from -1 to 4, as said below
Outputs:
- scores: float32 [8192, 1024], P(('groups', 'train'), 'test'), parts along dimension 0
The draws below stay inside these ranges and needn't reach their ends.
There are 2 independent parts, one for each index of `groups`. The reference program is written for one: setup_inputs(seed, part) draws one part's arguments, and reference() takes and returns one part's arrays. A program takes and returns all parts, laid end to end along the dimension named above; an argument that names none is the same for every part. Nothing has to cross between parts.
Inputs may be any that keep to these rules, and one draw needn't show every extreme that they name: `inverse_kernel`: symmetric.
All inputs are finite; a program needn't handle non-finite values.
Results may differ from the reference program's by a relative error of at most 0.0029.
Values may be sent and summed in bfloat16 or wider, within the bound.
A program may use at most 64 MiB of HBM per device.

```python
import jax
import jax.numpy as jnp

D = 4096
NTRAIN = 4096
NTEST = 1024


def draw_inverse_kernel(key, part):
    key = jax.random.fold_in(key, 11)
    key_diag = jax.random.fold_in(key, 1)
    key_off = jax.random.fold_in(key, 2)
    diag_vals = jnp.exp(jax.random.uniform(key_diag, (D,), jnp.float32, jnp.log(0.5), jnp.log(4.0)))
    noise = jnp.clip(jax.random.normal(key_off, (D, D), jnp.float32), -4.0, 4.0)
    symmetric = (noise + noise.T) * (0.9 / D ** 0.5)
    rows = jax.lax.broadcasted_iota(jnp.int32, (D, D), 0)
    cols = jax.lax.broadcasted_iota(jnp.int32, (D, D), 1)
    kernel = jnp.where(rows == cols, diag_vals[:, None], symmetric)
    return kernel.astype(jnp.bfloat16)


def block_scale(rng, dims, cuts, low, top_value):
    def one(axis_at, parts):
        draws = jax.random.uniform(jax.random.fold_in(jax.random.fold_in(rng, 6), axis_at), (parts,), jnp.float32, low / len(cuts), top_value / len(cuts))
        return jnp.repeat(jnp.exp(draws), dims[axis_at] // parts).reshape((-1,) + (1,) * (len(dims) - axis_at - 1))

    factor_of = one(*cuts[0])
    for cut in cuts[1:]:
        factor_of = factor_of * one(*cut)
    return factor_of


def normal_values(stream_key, dims, scale, limit, shards=(), dtype=jnp.bfloat16):
    entries = scale * jax.random.normal(stream_key, dims, jnp.float32)
    if shards:
        entries = entries * block_scale(stream_key, dims, shards, -0.22, 0.18)
    return jnp.clip(entries, -limit, limit).astype(dtype)


def setup_inputs(seed: int = 0, part: int = 0) -> dict:
    arg_keys = jax.random.split(jax.random.key(seed), 4)
    part_keys = jax.random.split(jax.random.fold_in(arg_keys[3], part), 4)
    train_feat = normal_values(part_keys[0], (NTRAIN, D), 1.0, 6.0, ((0, 4), (1, 4)))
    test_feat = normal_values(part_keys[1], (NTEST, D), 1.0, 6.0, ((0, 4), (1, 4)))
    inverse_kernel = draw_inverse_kernel(jax.random.fold_in(arg_keys[3], 71), part)
    return {"train_feat": train_feat, "test_feat": test_feat, "inverse_kernel": inverse_kernel}


def reference(train_feat, test_feat, inverse_kernel):
    precond = jnp.dot(test_feat, inverse_kernel, preferred_element_type=jnp.float32).astype(jnp.bfloat16)
    raw = jnp.dot(train_feat, precond.T, preferred_element_type=jnp.float32)
    return raw * (1.0 / (D ** 0.5))
```

```python
import functools

import jax
import jax.numpy as jnp
from jax import lax
from jax.experimental import pallas as pl
from jax.experimental.pallas import tpu as pltpu
from jax.sharding import PartitionSpec as P

MESH = pl.DeviceIdType.MESH
CORES = 2
LAST = (((1,), (1,)), ((), ()))


def kernel(nz, nt, chunks, train_ref, test_ref, inv_ref, out_ref,
           feats, pre, train_all, inv, acc,
           local_sem, inv_sem, z_send, z_recv, x_send, x_recv, c_send, c_recv):
    nx = nt // CORES
    z = lax.axis_index("train")
    s = lax.axis_index("test")
    x, core = s // CORES, s % CORES
    twin = {"test": x * CORES + 1 - core}
    rows, fz = test_ref.shape
    fs = train_ref.shape[1]
    part = rows // chunks
    up, down = {"train": z + 1}, {"train": z - 1}
    has_up, has_down = z < nz - 1, z > 0

    def as_int(flag):
        return jnp.where(flag, 1, 0)

    barrier = pltpu.get_barrier_semaphore()
    pl.semaphore_signal(barrier, inc=1, device_id=twin, device_id_type=MESH)
    links = 1 + as_int(has_up) + as_int(has_down) + as_int(x > 0) + as_int(x < nx - 1)

    @pl.when(has_up)
    def _():
        pl.semaphore_signal(barrier, inc=1, device_id=up, device_id_type=MESH)

    @pl.when(has_down)
    def _():
        pl.semaphore_signal(barrier, inc=1, device_id=down, device_id_type=MESH)

    @pl.when(x > 0)
    def _():
        pl.semaphore_signal(barrier, inc=1, device_id={"test": s - CORES}, device_id_type=MESH)

    @pl.when(x < nx - 1)
    def _():
        pl.semaphore_signal(barrier, inc=1, device_id={"test": s + CORES}, device_id_type=MESH)

    own_test = pltpu.make_async_copy(
        test_ref, feats.at[:, pl.ds(pl.multiple_of(z * fz, fz), fz)], local_sem.at[0])
    own_train = pltpu.make_async_copy(train_ref, train_all.at[s], local_sem.at[1])
    own_test.start()

    @pl.loop(0, nz)
    def _(j):
        pltpu.make_async_copy(
            inv_ref.at[:, pl.ds(pl.multiple_of(j * fz, fz), fz)], inv.at[j], inv_sem.at[j]).start()

    own_train.start()
    pl.semaphore_wait(barrier, links)

    def block(stream, c, j):
        buf = (feats, pre)[stream]
        return buf.at[pl.ds(c * part, part), pl.ds(pl.multiple_of(j * fz, fz), fz)]

    def z_copy(stream, c, h, way, first=False):
        j = z - h if way == 0 else z + h
        dst = block(stream, c, j)
        src = test_ref.at[pl.ds(c * part, part), :] if first and stream == 0 else dst
        return pltpu.make_async_remote_copy(
            src_ref=src, dst_ref=dst,
            send_sem=z_send.at[stream, way, c, h], recv_sem=z_recv.at[stream, way, c, h],
            device_id=up if way == 0 else down, device_id_type=MESH)

    def z_sends(h, way):
        return ((z >= h) & has_up) if way == 0 else ((z + h < nz) & has_down)

    def z_start(stream, c, h, first=False):
        for way in range(2):
            @pl.when(z_sends(h, way))
            def _():
                z_copy(stream, c, h, way, first).start()

    def z_wait_recv(stream, c, h, way):
        j = z - h if way == 0 else z + h
        dst = block(stream, c, j)
        pltpu.make_async_remote_copy(
            src_ref=dst, dst_ref=dst,
            send_sem=z_send.at[stream, way, c, h - 1], recv_sem=z_recv.at[stream, way, c, h - 1],
            device_id=down if way == 0 else up, device_id_type=MESH).wait_recv()

    def z_has(h, way):
        return (z >= h) if way == 0 else (z + h < nz)

    def x_copy(h, way):
        owner = s - CORES * h if way == 0 else s + CORES * h
        return pltpu.make_async_remote_copy(
            src_ref=train_ref if h == 0 else train_all.at[owner], dst_ref=train_all.at[owner],
            send_sem=x_send.at[way, h], recv_sem=x_recv.at[way, h],
            device_id={"test": s + CORES if way == 0 else s - CORES}, device_id_type=MESH)

    def x_has(h, way):
        return (x >= h) if way == 0 else (x + h < nx)

    def x_sends(h, way):
        return x_has(h, way) & ((x < nx - 1) if way == 0 else (x > 0))

    def x_wait_recv(h, way):
        owner = s - CORES * h if way == 0 else s + CORES * h
        pltpu.make_async_remote_copy(
            src_ref=train_all.at[owner], dst_ref=train_all.at[owner],
            send_sem=x_send.at[way, h - 1], recv_sem=x_recv.at[way, h - 1],
            device_id={"test": s - CORES if way == 0 else s + CORES}, device_id_type=MESH).wait_recv()

    def twin_copy(h, way, mine=True):
        c = core if mine else 1 - core
        owner = (x - h if way == 0 else x + h) * CORES + c
        return pltpu.make_async_remote_copy(
            src_ref=train_ref if h == 0 else train_all.at[owner], dst_ref=train_all.at[owner],
            send_sem=c_send.at[way, h], recv_sem=c_recv.at[way, h],
            device_id=twin, device_id_type=MESH)

    def precond(c, h):
        for way in range(2):
            @pl.when(z_has(h, way))
            def _():
                j = z - h if way == 0 else z + h
                acc[...] += lax.dot_general(
                    block(0, c, j)[...], inv[j], LAST, preferred_element_type=jnp.float32)

    def step(i):
        t, p = i < chunks, i >= 1
        if t:
            z_start(0, i, 0, True)
        if p:
            z_start(1, i - 1, 0)
        if i == 0:
            for way in range(2):
                @pl.when(x_sends(0, way))
                def _():
                    x_copy(0, way).start()
            twin_copy(0, 0).start()
            own_test.wait()

            @pl.loop(0, nz)
            def _(j):
                pltpu.make_async_copy(
                    inv_ref.at[:, pl.ds(pl.multiple_of(j * fz, fz), fz)], inv.at[j], inv_sem.at[j]).wait()
        if i == chunks:
            own_train.wait()
            for h in range(1, nx):
                for way in range(2):
                    @pl.when(x_has(h, way))
                    def _():
                        x_wait_recv(h, way)

                        @pl.when(x_sends(h, way))
                        def _():
                            x_copy(h, way).start()

                        twin_copy(h, way).start()
        if t:
            acc[...] = lax.dot_general(
                block(0, i, z)[...], inv[z], LAST, preferred_element_type=jnp.float32)

        @pl.loop(1, nz)
        def _(h):
            for stream, c, on in ((0, i, t), (1, i - 1, p)):
                if not on:
                    continue
                for way in range(2):
                    @pl.when(z_has(h, way))
                    def _():
                        z_wait_recv(stream, c, h, way)

                        @pl.when(z_sends(h, way))
                        def _():
                            z_copy(stream, c, h, way).start()
            if t:
                precond(i, h)

        if t:
            block(1, i, z)[...] = acc[...].astype(jnp.bfloat16)

    for i in range(chunks + 1):
        step(i)

    twin_copy(0, 0, False).wait_recv()
    for h in range(1, nx):
        for way in range(2):
            @pl.when(x_has(h, way))
            def _():
                twin_copy(h, way, False).wait_recv()

    scale = 1.0 / (fz * nz) ** 0.5
    total = jnp.zeros(out_ref.shape, jnp.float32)
    for k in range(nt):
        total += lax.dot_general(
            train_all[k], pre[:, k * fs:(k + 1) * fs], LAST, preferred_element_type=jnp.float32)
    out_ref[...] = total * scale

    twin_copy(0, 0).wait_send()
    for h in range(nx):
        for way in range(2):
            @pl.when(x_sends(h, way))
            def _():
                x_copy(h, way).wait_send()
            if h > 0:
                @pl.when(x_has(h, way))
                def _():
                    twin_copy(h, way).wait_send()
    for c in range(chunks):
        for stream in range(2):
            @pl.loop(0, nz)
            def _(h):
                for way in range(2):
                    @pl.when(z_sends(h, way))
                    def _():
                        z_copy(stream, c, h, way).wait_send()


def shards(nz, nt, train_feat, test_feat, inverse_kernel):
    chunks = 4
    rows, fz = test_feat.shape
    train_rows, fs = train_feat.shape
    d = fz * nz
    nx = nt // CORES
    dma = pltpu.SemaphoreType.DMA
    anywhere = pl.BlockSpec(memory_space=pl.ANY)
    return pl.pallas_call(
        functools.partial(kernel, nz, nt, chunks),
        out_shape=jax.ShapeDtypeStruct((train_rows, rows), jnp.float32),
        in_specs=[anywhere] * 3,
        out_specs=pl.BlockSpec(memory_space=pltpu.VMEM),
        scratch_shapes=[
            pltpu.VMEM((rows, d), jnp.bfloat16),
            pltpu.VMEM((rows, d), jnp.bfloat16),
            pltpu.VMEM((nt, train_rows, fs), jnp.bfloat16),
            pltpu.VMEM((nz, fz, fz), jnp.bfloat16),
            pltpu.VMEM((rows // chunks, fz), jnp.float32),
            dma((2,)),
            dma((nz,)),
            dma((2, 2, chunks, nz)),
            dma((2, 2, chunks, nz)),
            dma((2, nx)),
            dma((2, nx)),
            dma((2, nx)),
            dma((2, nx)),
        ],
        compiler_params=pltpu.CompilerParams(
            collective_id=0, has_side_effects=True, vmem_limit_bytes=56 * 1024 * 1024),
        cost_estimate=pl.CostEstimate(
            flops=2 * rows * d * (fz + train_rows), bytes_accessed=16 * 2 ** 20, transcendentals=0),
    )(train_feat, test_feat, inverse_kernel)


def solution(mesh):
    placed = (P(("groups", "train"), "test"), P(("groups", "test"), "train"), P("train", None))
    return jax.shard_map(
        functools.partial(shards, mesh.shape["train"], mesh.shape["test"]),
        mesh=mesh,
        in_specs=placed,
        out_specs=P(("groups", "train"), "test"),
        check_vma=False,
    )
```

```python
import functools

import jax
import jax.numpy as jnp
from jax import lax
from jax.experimental import pallas as pl
from jax.experimental.pallas import tpu as pltpu
from jax.sharding import PartitionSpec as P

MESH = pl.DeviceIdType.MESH
CORES = 2
LAST = (((1,), (1,)), ((), ()))


def kernel(nz, nt, chunks, train_ref, test_ref, inv_ref, out_ref,
           feats, pre, train_all, inv, acc, terms, sum_in, sum_out,
           local_sem, inv_sem, z_send, z_recv, x_send, x_recv, c_send, c_recv, s_send, s_recv):
    nx = nt // CORES
    z = lax.axis_index("train")
    s = lax.axis_index("test")
    x, core = s // CORES, s % CORES
    twin = {"test": x * CORES + 1 - core}
    rows, fz = test_ref.shape
    fs = train_ref.shape[1]
    part = rows // chunks
    scale = 1.0 / (fz * nz) ** 0.5
    up, down = {"train": z + 1}, {"train": z - 1}
    has_up, has_down = z < nz - 1, z > 0

    def as_int(flag):
        return jnp.where(flag, 1, 0)

    barrier = pltpu.get_barrier_semaphore()
    pl.semaphore_signal(barrier, inc=1, device_id=twin, device_id_type=MESH)
    links = 1 + as_int(has_up) + as_int(has_down) + as_int(x > 0) + as_int(x < nx - 1)

    @pl.when(has_up)
    def _():
        pl.semaphore_signal(barrier, inc=1, device_id=up, device_id_type=MESH)

    @pl.when(has_down)
    def _():
        pl.semaphore_signal(barrier, inc=1, device_id=down, device_id_type=MESH)

    @pl.when(x > 0)
    def _():
        pl.semaphore_signal(barrier, inc=1, device_id={"test": s - CORES}, device_id_type=MESH)

    @pl.when(x < nx - 1)
    def _():
        pl.semaphore_signal(barrier, inc=1, device_id={"test": s + CORES}, device_id_type=MESH)

    own_test = pltpu.make_async_copy(
        test_ref, feats.at[:, pl.ds(pl.multiple_of(z * fz, fz), fz)], local_sem.at[0])
    own_train = pltpu.make_async_copy(train_ref, train_all.at[s], local_sem.at[1])
    own_test.start()

    @pl.loop(0, nz)
    def _(j):
        pltpu.make_async_copy(
            inv_ref.at[:, pl.ds(pl.multiple_of(j * fz, fz), fz)], inv.at[j], inv_sem.at[j]).start()

    own_train.start()
    pl.semaphore_wait(barrier, links)

    def block(stream, c, j):
        buf = (feats, pre)[stream]
        return buf.at[pl.ds(c * part, part), pl.ds(pl.multiple_of(j * fz, fz), fz)]

    def z_copy(stream, c, h, way, first=False):
        j = z - h if way == 0 else z + h
        dst = block(stream, c, j)
        src = test_ref.at[pl.ds(c * part, part), :] if first and stream == 0 else dst
        return pltpu.make_async_remote_copy(
            src_ref=src, dst_ref=dst,
            send_sem=z_send.at[stream, way, c, h], recv_sem=z_recv.at[stream, way, c, h],
            device_id=up if way == 0 else down, device_id_type=MESH)

    def z_sends(h, way):
        return ((z >= h) & has_up) if way == 0 else ((z + h < nz) & has_down)

    def z_start(stream, c, h, first=False):
        for way in range(2):
            @pl.when(z_sends(h, way))
            def _():
                z_copy(stream, c, h, way, first).start()

    def z_wait_recv(stream, c, h, way):
        j = z - h if way == 0 else z + h
        dst = block(stream, c, j)
        pltpu.make_async_remote_copy(
            src_ref=dst, dst_ref=dst,
            send_sem=z_send.at[stream, way, c, h - 1], recv_sem=z_recv.at[stream, way, c, h - 1],
            device_id=down if way == 0 else up, device_id_type=MESH).wait_recv()

    def z_has(h, way):
        return (z >= h) if way == 0 else (z + h < nz)

    def x_copy(h, way):
        owner = s - CORES * h if way == 0 else s + CORES * h
        return pltpu.make_async_remote_copy(
            src_ref=train_ref if h == 0 else train_all.at[owner], dst_ref=train_all.at[owner],
            send_sem=x_send.at[way, h], recv_sem=x_recv.at[way, h],
            device_id={"test": s + CORES if way == 0 else s - CORES}, device_id_type=MESH)

    def x_has(h, way):
        return (x >= h) if way == 0 else (x + h < nx)

    def x_sends(h, way):
        return x_has(h, way) & ((x < nx - 1) if way == 0 else (x > 0))

    def x_wait_recv(h, way):
        owner = s - CORES * h if way == 0 else s + CORES * h
        pltpu.make_async_remote_copy(
            src_ref=train_all.at[owner], dst_ref=train_all.at[owner],
            send_sem=x_send.at[way, h - 1], recv_sem=x_recv.at[way, h - 1],
            device_id={"test": s - CORES if way == 0 else s + CORES}, device_id_type=MESH).wait_recv()

    def twin_copy(h, way, mine=True):
        c = core if mine else 1 - core
        owner = (x - h if way == 0 else x + h) * CORES + c
        return pltpu.make_async_remote_copy(
            src_ref=train_ref if h == 0 else train_all.at[owner], dst_ref=train_all.at[owner],
            send_sem=c_send.at[way, h], recv_sem=c_recv.at[way, h],
            device_id=twin, device_id_type=MESH)

    def score(h, way):
        j = z - h if way == 0 else z + h
        at = j * fz
        cols = pl.ds(pl.multiple_of(at % fs, fz), fz)
        out_ref[...] += lax.dot_general(
            train_all[at // fs, :, cols], pre[:, pl.ds(pl.multiple_of(at, fz), fz)], LAST,
            preferred_element_type=jnp.float32) * scale

    def sum_copy(way, k):
        return pltpu.make_async_remote_copy(
            src_ref=sum_out.at[way, k], dst_ref=sum_in.at[way, k],
            send_sem=s_send.at[way, k], recv_sem=s_recv.at[way, k],
            device_id=up if way == 0 else down, device_id_type=MESH)

    def sum_sends(k, way):
        return (nz - 1 - k > z) if way == 0 else (k < z)

    def sum_gets(k, way):
        return ((nz - 1 - k >= z) & has_down) if way == 0 else ((k <= z) & has_up)

    def sum_step(k):
        for way in range(2):
            j = nz - 1 - k if way == 0 else k

            @pl.when(sum_gets(k, way))
            def _():
                sum_copy(way, k).wait_recv()

                @pl.when(j != z)
                def _():
                    sum_out[way, k] = (terms[j] + sum_in[way, k].astype(jnp.float32)).astype(jnp.bfloat16)

                @pl.when(j == z)
                def _():
                    terms[z] += sum_in[way, k].astype(jnp.float32)

            @pl.when(sum_sends(k, way))
            def _():
                @pl.when(jnp.logical_not(sum_gets(k, way)))
                def _():
                    sum_out[way, k] = terms[j].astype(jnp.bfloat16)

                sum_copy(way, k).start()

    def z_pass(stream, c, h):
        for way in range(2):
            @pl.when(z_has(h, way))
            def _():
                z_wait_recv(stream, c, h, way)

                @pl.when(z_sends(h, way))
                def _():
                    z_copy(stream, c, h, way).start()

    z_start(0, 0, 0, True)
    for way in range(2):
        @pl.when(x_sends(0, way))
        def _():
            x_copy(0, way).start()
    twin_copy(0, 0).start()
    own_test.wait()

    @pl.loop(0, nz)
    def _(j):
        pltpu.make_async_copy(
            inv_ref.at[:, pl.ds(pl.multiple_of(j * fz, fz), fz)], inv.at[j], inv_sem.at[j]).wait()

    def term(j):
        terms[j] = jnp.dot(block(0, 1, z)[...], inv[j], preferred_element_type=jnp.float32)

    @pl.loop(0, nz)
    def _(k):
        term(jnp.where(k % 2 == 0, nz - 1 - k // 2, k // 2))

    sum_step(0)
    acc[...] = lax.dot_general(
        block(0, 0, z)[...], inv[z], LAST, preferred_element_type=jnp.float32)

    @pl.loop(1, nz)
    def _(h):
        z_pass(0, 0, h)
        sum_step(h)
        for way in range(2):
            @pl.when(z_has(h, way))
            def _():
                j = z - h if way == 0 else z + h
                acc[...] += lax.dot_general(
                    block(0, 0, j)[...], inv[j], LAST, preferred_element_type=jnp.float32)

    block(1, 0, z)[...] = acc[...].astype(jnp.bfloat16)
    z_start(1, 0, 0)
    block(1, 1, z)[...] = terms[z].astype(jnp.bfloat16)
    z_start(1, 1, 0)

    @pl.loop(1, nz - 1)
    def _(h):
        z_pass(1, 0, h)
        z_pass(1, 1, h)

    own_train.wait()
    for h in range(1, nx):
        for way in range(2):
            @pl.when(x_has(h, way))
            def _():
                x_wait_recv(h, way)

                @pl.when(x_sends(h, way))
                def _():
                    x_copy(h, way).start()

                twin_copy(h, way).start()
    twin_copy(0, 0, False).wait_recv()
    for h in range(1, nx):
        for way in range(2):
            @pl.when(x_has(h, way))
            def _():
                twin_copy(h, way, False).wait_recv()

    out_ref[...] = jnp.zeros(out_ref.shape, jnp.float32)
    score(0, 0)

    @pl.loop(1, nz - 1)
    def _(h):
        for way in range(2):
            @pl.when(z_has(h, way))
            def _():
                score(h, way)

    z_pass(1, 0, nz - 1)
    z_pass(1, 1, nz - 1)
    for way in range(2):
        @pl.when(z_has(nz - 1, way))
        def _():
            score(nz - 1, way)

    twin_copy(0, 0).wait_send()
    for h in range(nx):
        for way in range(2):
            @pl.when(x_sends(h, way))
            def _():
                x_copy(h, way).wait_send()
            if h > 0:
                @pl.when(x_has(h, way))
                def _():
                    twin_copy(h, way).wait_send()

    @pl.loop(0, nz)
    def _(h):
        for way in range(2):
            for stream, c in ((0, 0), (1, 0), (1, 1)):
                @pl.when(z_sends(h, way))
                def _():
                    z_copy(stream, c, h, way).wait_send()

            @pl.when(sum_sends(h, way))
            def _():
                sum_copy(way, h).wait_send()


def shards(nz, nt, train_feat, test_feat, inverse_kernel):
    chunks = 2
    rows, fz = test_feat.shape
    train_rows, fs = train_feat.shape
    d = fz * nz
    nx = nt // CORES
    dma = pltpu.SemaphoreType.DMA
    anywhere = pl.BlockSpec(memory_space=pl.ANY)
    return pl.pallas_call(
        functools.partial(kernel, nz, nt, chunks),
        out_shape=jax.ShapeDtypeStruct((train_rows, rows), jnp.float32),
        in_specs=[anywhere] * 3,
        out_specs=pl.BlockSpec(memory_space=pltpu.VMEM),
        scratch_shapes=[
            pltpu.VMEM((rows, d), jnp.bfloat16),
            pltpu.VMEM((rows, d), jnp.bfloat16),
            pltpu.VMEM((nt, train_rows, fs), jnp.bfloat16),
            pltpu.VMEM((nz, fz, fz), jnp.bfloat16),
            pltpu.VMEM((rows // chunks, fz), jnp.float32),
            pltpu.VMEM((nz, rows // chunks, fz), jnp.float32),
            pltpu.VMEM((2, nz, rows // chunks, fz), jnp.bfloat16),
            pltpu.VMEM((2, nz, rows // chunks, fz), jnp.bfloat16),
            dma((2,)),
            dma((nz,)),
            dma((2, 2, chunks, nz)),
            dma((2, 2, chunks, nz)),
            dma((2, nx)),
            dma((2, nx)),
            dma((2, nx)),
            dma((2, nx)),
            dma((2, nz)),
            dma((2, nz)),
        ],
        compiler_params=pltpu.CompilerParams(
            collective_id=0, has_side_effects=True, vmem_limit_bytes=56 * 1024 * 1024),
        cost_estimate=pl.CostEstimate(
            flops=2 * rows * d * (fz + train_rows), bytes_accessed=16 * 2 ** 20, transcendentals=0),
    )(train_feat, test_feat, inverse_kernel)


def solution(mesh):
    placed = (P(("groups", "train"), "test"), P(("groups", "test"), "train"), P("train", None))
    return jax.shard_map(
        functools.partial(shards, mesh.shape["train"], mesh.shape["test"]),
        mesh=mesh,
        in_specs=placed,
        out_specs=P(("groups", "train"), "test"),
        check_vma=False,
    )
```

```python
import functools

import jax
import jax.numpy as jnp
from jax import lax
from jax.experimental import pallas as pl
from jax.experimental.pallas import tpu as pltpu
from jax.sharding import PartitionSpec as P

MESH = pl.DeviceIdType.MESH
CORES = 2
LAST = (((1,), (1,)), ((), ()))


def kernel(nz, nt, chunks, train_ref, test_ref, inv_ref, out_ref,
           feats, pre, train_all, inv, acc, terms, sum_in, sum_out,
           local_sem, inv_sem, z_send, z_recv, x_send, x_recv, c_send, c_recv, s_send, s_recv):
    nx = nt // CORES
    z = lax.axis_index("train")
    s = lax.axis_index("test")
    x, core = s // CORES, s % CORES
    twin = {"test": x * CORES + 1 - core}
    rows, fz = test_ref.shape
    fs = train_ref.shape[1]
    part = rows // chunks
    scale = 1.0 / (fz * nz) ** 0.5
    up, down = {"train": z + 1}, {"train": z - 1}
    has_up, has_down = z < nz - 1, z > 0

    def as_int(flag):
        return jnp.where(flag, 1, 0)

    barrier = pltpu.get_barrier_semaphore()
    pl.semaphore_signal(barrier, inc=1, device_id=twin, device_id_type=MESH)
    links = 1 + as_int(has_up) + as_int(has_down) + as_int(x > 0) + as_int(x < nx - 1)

    @pl.when(has_up)
    def _():
        pl.semaphore_signal(barrier, inc=1, device_id=up, device_id_type=MESH)

    @pl.when(has_down)
    def _():
        pl.semaphore_signal(barrier, inc=1, device_id=down, device_id_type=MESH)

    @pl.when(x > 0)
    def _():
        pl.semaphore_signal(barrier, inc=1, device_id={"test": s - CORES}, device_id_type=MESH)

    @pl.when(x < nx - 1)
    def _():
        pl.semaphore_signal(barrier, inc=1, device_id={"test": s + CORES}, device_id_type=MESH)

    own_test = pltpu.make_async_copy(
        test_ref, feats.at[:, pl.ds(pl.multiple_of(z * fz, fz), fz)], local_sem.at[0])
    own_train = pltpu.make_async_copy(train_ref, train_all.at[s], local_sem.at[1])
    own_test.start()

    @pl.loop(0, nz)
    def _(j):
        pltpu.make_async_copy(
            inv_ref.at[:, pl.ds(pl.multiple_of(j * fz, fz), fz)], inv.at[j], inv_sem.at[j]).start()

    own_train.start()
    pl.semaphore_wait(barrier, links)

    def block(stream, c, j):
        buf = (feats, pre)[stream]
        return buf.at[pl.ds(c * part, part), pl.ds(pl.multiple_of(j * fz, fz), fz)]

    def z_copy(stream, c, h, way, first=False):
        j = z - h if way == 0 else z + h
        dst = block(stream, c, j)
        src = test_ref.at[pl.ds(c * part, part), :] if first and stream == 0 else dst
        return pltpu.make_async_remote_copy(
            src_ref=src, dst_ref=dst,
            send_sem=z_send.at[stream, way, c, h], recv_sem=z_recv.at[stream, way, c, h],
            device_id=up if way == 0 else down, device_id_type=MESH)

    def z_sends(h, way):
        return ((z >= h) & has_up) if way == 0 else ((z + h < nz) & has_down)

    def z_start(stream, c, h, first=False):
        for way in range(2):
            @pl.when(z_sends(h, way))
            def _():
                z_copy(stream, c, h, way, first).start()

    def z_wait_recv(stream, c, h, way):
        j = z - h if way == 0 else z + h
        dst = block(stream, c, j)
        pltpu.make_async_remote_copy(
            src_ref=dst, dst_ref=dst,
            send_sem=z_send.at[stream, way, c, h - 1], recv_sem=z_recv.at[stream, way, c, h - 1],
            device_id=down if way == 0 else up, device_id_type=MESH).wait_recv()

    def z_has(h, way):
        return (z >= h) if way == 0 else (z + h < nz)

    def x_copy(h, way):
        owner = s - CORES * h if way == 0 else s + CORES * h
        return pltpu.make_async_remote_copy(
            src_ref=train_ref if h == 0 else train_all.at[owner], dst_ref=train_all.at[owner],
            send_sem=x_send.at[way, h], recv_sem=x_recv.at[way, h],
            device_id={"test": s + CORES if way == 0 else s - CORES}, device_id_type=MESH)

    def x_has(h, way):
        return (x >= h) if way == 0 else (x + h < nx)

    def x_sends(h, way):
        return x_has(h, way) & ((x < nx - 1) if way == 0 else (x > 0))

    def x_wait_recv(h, way):
        owner = s - CORES * h if way == 0 else s + CORES * h
        pltpu.make_async_remote_copy(
            src_ref=train_all.at[owner], dst_ref=train_all.at[owner],
            send_sem=x_send.at[way, h - 1], recv_sem=x_recv.at[way, h - 1],
            device_id={"test": s - CORES if way == 0 else s + CORES}, device_id_type=MESH).wait_recv()

    def twin_copy(h, way, mine=True):
        c = core if mine else 1 - core
        owner = (x - h if way == 0 else x + h) * CORES + c
        return pltpu.make_async_remote_copy(
            src_ref=train_ref if h == 0 else train_all.at[owner], dst_ref=train_all.at[owner],
            send_sem=c_send.at[way, h], recv_sem=c_recv.at[way, h],
            device_id=twin, device_id_type=MESH)

    def score(h, way):
        j = z - h if way == 0 else z + h
        at = j * fz
        cols = pl.ds(pl.multiple_of(at % fs, fz), fz)
        out_ref[...] += lax.dot_general(
            train_all[at // fs, :, cols], pre[:, pl.ds(pl.multiple_of(at, fz), fz)], LAST,
            preferred_element_type=jnp.float32) * scale

    def sum_copy(way, k):
        return pltpu.make_async_remote_copy(
            src_ref=sum_out.at[way, k], dst_ref=sum_in.at[way, k],
            send_sem=s_send.at[way, k], recv_sem=s_recv.at[way, k],
            device_id=up if way == 0 else down, device_id_type=MESH)

    def sum_sends(k, way):
        return (nz - 1 - k > z) if way == 0 else (k < z)

    def sum_gets(k, way):
        return ((nz - 1 - k >= z) & has_down) if way == 0 else ((k <= z) & has_up)

    def sum_step(at):
        for way in range(2):
            k = at - z if way == 0 else at - (nz - 1 - z)
            j = nz - 1 - k if way == 0 else k

            @pl.when((k >= 0) & sum_gets(k, way))
            def _():
                sum_copy(way, k).wait_recv()

                @pl.when(j != z)
                def _():
                    sum_out[way, k] = (terms[j] + sum_in[way, k].astype(jnp.float32)).astype(jnp.bfloat16)

                @pl.when(j == z)
                def _():
                    terms[z] += sum_in[way, k].astype(jnp.float32)

            @pl.when((k >= 0) & sum_sends(k, way))
            def _():
                @pl.when(jnp.logical_not(sum_gets(k, way)))
                def _():
                    sum_out[way, k] = terms[j].astype(jnp.bfloat16)

                sum_copy(way, k).start()

    def z_pass(stream, c, h):
        for way in range(2):
            @pl.when(z_has(h, way))
            def _():
                z_wait_recv(stream, c, h, way)

                @pl.when(z_sends(h, way))
                def _():
                    z_copy(stream, c, h, way).start()

    z_start(0, 0, 0, True)
    for way in range(2):
        @pl.when(x_sends(0, way))
        def _():
            x_copy(0, way).start()
    twin_copy(0, 0).start()
    own_test.wait()

    @pl.loop(0, nz)
    def _(j):
        pltpu.make_async_copy(
            inv_ref.at[:, pl.ds(pl.multiple_of(j * fz, fz), fz)], inv.at[j], inv_sem.at[j]).wait()

    def term(j):
        terms[j] = jnp.dot(block(0, 1, z)[...], inv[j], preferred_element_type=jnp.float32)

    @pl.loop(0, nz)
    def _(k):
        term(jnp.where(k % 2 == 0, nz - 1 - k // 2, k // 2))

    sum_step(0)
    acc[...] = lax.dot_general(
        block(0, 0, z)[...], inv[z], LAST, preferred_element_type=jnp.float32)

    def precond(h):
        for way in range(2):
            @pl.when(z_has(h, way))
            def _():
                j = z - h if way == 0 else z + h
                acc[...] += lax.dot_general(
                    block(0, 0, j)[...], inv[j], LAST, preferred_element_type=jnp.float32)

    @pl.loop(1, nz - 1)
    def _(h):
        z_pass(0, 0, h)
        sum_step(h)
        precond(h)

    z_pass(0, 0, nz - 1)
    precond(nz - 1)
    block(1, 0, z)[...] = acc[...].astype(jnp.bfloat16)
    z_start(1, 0, 0)
    sum_step(nz - 1)
    block(1, 1, z)[...] = terms[z].astype(jnp.bfloat16)
    z_start(1, 1, 0)

    @pl.loop(1, nz - 1)
    def _(h):
        z_pass(1, 0, h)
        z_pass(1, 1, h)

    own_train.wait()
    for h in range(1, nx):
        for way in range(2):
            @pl.when(x_has(h, way))
            def _():
                x_wait_recv(h, way)

                @pl.when(x_sends(h, way))
                def _():
                    x_copy(h, way).start()

                twin_copy(h, way).start()
    twin_copy(0, 0, False).wait_recv()
    for h in range(1, nx):
        for way in range(2):
            @pl.when(x_has(h, way))
            def _():
                twin_copy(h, way, False).wait_recv()

    out_ref[...] = jnp.zeros(out_ref.shape, jnp.float32)
    score(0, 0)

    @pl.loop(1, nz - 1)
    def _(h):
        for way in range(2):
            @pl.when(z_has(h, way))
            def _():
                score(h, way)

    z_pass(1, 0, nz - 1)
    z_pass(1, 1, nz - 1)
    for way in range(2):
        @pl.when(z_has(nz - 1, way))
        def _():
            score(nz - 1, way)

    twin_copy(0, 0).wait_send()
    for h in range(nx):
        for way in range(2):
            @pl.when(x_sends(h, way))
            def _():
                x_copy(h, way).wait_send()
            if h > 0:
                @pl.when(x_has(h, way))
                def _():
                    twin_copy(h, way).wait_send()

    @pl.loop(0, nz)
    def _(h):
        for way in range(2):
            for stream, c in ((0, 0), (1, 0), (1, 1)):
                @pl.when(z_sends(h, way))
                def _():
                    z_copy(stream, c, h, way).wait_send()

            @pl.when(sum_sends(h, way))
            def _():
                sum_copy(way, h).wait_send()


def shards(nz, nt, train_feat, test_feat, inverse_kernel):
    chunks = 2
    rows, fz = test_feat.shape
    train_rows, fs = train_feat.shape
    d = fz * nz
    nx = nt // CORES
    dma = pltpu.SemaphoreType.DMA
    anywhere = pl.BlockSpec(memory_space=pl.ANY)
    return pl.pallas_call(
        functools.partial(kernel, nz, nt, chunks),
        out_shape=jax.ShapeDtypeStruct((train_rows, rows), jnp.float32),
        in_specs=[anywhere] * 3,
        out_specs=pl.BlockSpec(memory_space=pltpu.VMEM),
        scratch_shapes=[
            pltpu.VMEM((rows, d), jnp.bfloat16),
            pltpu.VMEM((rows, d), jnp.bfloat16),
            pltpu.VMEM((nt, train_rows, fs), jnp.bfloat16),
            pltpu.VMEM((nz, fz, fz), jnp.bfloat16),
            pltpu.VMEM((rows // chunks, fz), jnp.float32),
            pltpu.VMEM((nz, rows // chunks, fz), jnp.float32),
            pltpu.VMEM((2, nz, rows // chunks, fz), jnp.bfloat16),
            pltpu.VMEM((2, nz, rows // chunks, fz), jnp.bfloat16),
            dma((2,)),
            dma((nz,)),
            dma((2, 2, chunks, nz)),
            dma((2, 2, chunks, nz)),
            dma((2, nx)),
            dma((2, nx)),
            dma((2, nx)),
            dma((2, nx)),
            dma((2, nz)),
            dma((2, nz)),
        ],
        compiler_params=pltpu.CompilerParams(
            collective_id=0, has_side_effects=True, vmem_limit_bytes=56 * 1024 * 1024),
        cost_estimate=pl.CostEstimate(
            flops=2 * rows * d * (fz + train_rows), bytes_accessed=16 * 2 ** 20, transcendentals=0),
    )(train_feat, test_feat, inverse_kernel)


def solution(mesh):
    placed = (P(("groups", "train"), "test"), P(("groups", "test"), "train"), P("train", None))
    return jax.shard_map(
        functools.partial(shards, mesh.shape["train"], mesh.shape["test"]),
        mesh=mesh,
        in_specs=placed,
        out_specs=P(("groups", "train"), "test"),
        check_vma=False,
    )
```

```python
import functools

import jax
import jax.numpy as jnp
from jax import lax
from jax.experimental import pallas as pl
from jax.experimental.pallas import tpu as pltpu
from jax.sharding import PartitionSpec as P

MESH = pl.DeviceIdType.MESH
CORES = 2
LAST = (((1,), (1,)), ((), ()))


def kernel(nz, nt, chunks, train_ref, test_ref, inv_ref, out_ref,
           feats, pre, train_all, inv, acc, terms, sum_in, sum_out,
           local_sem, inv_sem, z_send, z_recv, x_send, x_recv, c_send, c_recv, s_send, s_recv):
    nx = nt // CORES
    z = lax.axis_index("train")
    s = lax.axis_index("test")
    x, core = s // CORES, s % CORES
    twin = {"test": x * CORES + 1 - core}
    rows, fz = test_ref.shape
    fs = train_ref.shape[1]
    part = rows // chunks
    scale = 1.0 / (fz * nz) ** 0.5
    up, down = {"train": z + 1}, {"train": z - 1}
    has_up, has_down = z < nz - 1, z > 0

    def as_int(flag):
        return jnp.where(flag, 1, 0)

    barrier = pltpu.get_barrier_semaphore()
    pl.semaphore_signal(barrier, inc=1, device_id=twin, device_id_type=MESH)
    links = 1 + as_int(has_up) + as_int(has_down) + as_int(x > 0) + as_int(x < nx - 1)

    @pl.when(has_up)
    def _():
        pl.semaphore_signal(barrier, inc=1, device_id=up, device_id_type=MESH)

    @pl.when(has_down)
    def _():
        pl.semaphore_signal(barrier, inc=1, device_id=down, device_id_type=MESH)

    @pl.when(x > 0)
    def _():
        pl.semaphore_signal(barrier, inc=1, device_id={"test": s - CORES}, device_id_type=MESH)

    @pl.when(x < nx - 1)
    def _():
        pl.semaphore_signal(barrier, inc=1, device_id={"test": s + CORES}, device_id_type=MESH)

    own_test = pltpu.make_async_copy(
        test_ref, feats.at[:, pl.ds(pl.multiple_of(z * fz, fz), fz)], local_sem.at[0])
    own_train = pltpu.make_async_copy(train_ref, train_all.at[s], local_sem.at[1])
    own_test.start()

    @pl.loop(0, nz)
    def _(j):
        pltpu.make_async_copy(
            inv_ref.at[:, pl.ds(pl.multiple_of(j * fz, fz), fz)], inv.at[j], inv_sem.at[j]).start()

    own_train.start()
    pl.semaphore_wait(barrier, links)

    def block(stream, c, j):
        buf = (feats, pre)[stream]
        return buf.at[pl.ds(c * part, part), pl.ds(pl.multiple_of(j * fz, fz), fz)]

    def z_copy(stream, c, h, way, first=False):
        j = z - h if way == 0 else z + h
        dst = block(stream, c, j)
        src = test_ref.at[pl.ds(c * part, part), :] if first and stream == 0 else dst
        return pltpu.make_async_remote_copy(
            src_ref=src, dst_ref=dst,
            send_sem=z_send.at[stream, way, c, h], recv_sem=z_recv.at[stream, way, c, h],
            device_id=up if way == 0 else down, device_id_type=MESH)

    def z_sends(h, way):
        return ((z >= h) & has_up) if way == 0 else ((z + h < nz) & has_down)

    def z_start(stream, c, h, first=False):
        for way in range(2):
            @pl.when(z_sends(h, way))
            def _():
                z_copy(stream, c, h, way, first).start()

    def z_wait_recv(stream, c, h, way):
        j = z - h if way == 0 else z + h
        dst = block(stream, c, j)
        pltpu.make_async_remote_copy(
            src_ref=dst, dst_ref=dst,
            send_sem=z_send.at[stream, way, c, h - 1], recv_sem=z_recv.at[stream, way, c, h - 1],
            device_id=down if way == 0 else up, device_id_type=MESH).wait_recv()

    def z_has(h, way):
        return (z >= h) if way == 0 else (z + h < nz)

    def x_copy(h, way):
        owner = s - CORES * h if way == 0 else s + CORES * h
        return pltpu.make_async_remote_copy(
            src_ref=train_ref if h == 0 else train_all.at[owner], dst_ref=train_all.at[owner],
            send_sem=x_send.at[way, h], recv_sem=x_recv.at[way, h],
            device_id={"test": s + CORES if way == 0 else s - CORES}, device_id_type=MESH)

    def x_has(h, way):
        return (x >= h) if way == 0 else (x + h < nx)

    def x_sends(h, way):
        return x_has(h, way) & ((x < nx - 1) if way == 0 else (x > 0))

    def x_wait_recv(h, way):
        owner = s - CORES * h if way == 0 else s + CORES * h
        pltpu.make_async_remote_copy(
            src_ref=train_all.at[owner], dst_ref=train_all.at[owner],
            send_sem=x_send.at[way, h - 1], recv_sem=x_recv.at[way, h - 1],
            device_id={"test": s - CORES if way == 0 else s + CORES}, device_id_type=MESH).wait_recv()

    def twin_copy(h, way, mine=True):
        c = core if mine else 1 - core
        owner = (x - h if way == 0 else x + h) * CORES + c
        return pltpu.make_async_remote_copy(
            src_ref=train_ref if h == 0 else train_all.at[owner], dst_ref=train_all.at[owner],
            send_sem=c_send.at[way, h], recv_sem=c_recv.at[way, h],
            device_id=twin, device_id_type=MESH)

    def score(h, way):
        j = z - h if way == 0 else z + h
        at = j * fz
        cols = pl.ds(pl.multiple_of(at % fs, fz), fz)
        out_ref[...] += lax.dot_general(
            train_all[at // fs, :, cols], pre[:, pl.ds(pl.multiple_of(at, fz), fz)], LAST,
            preferred_element_type=jnp.float32) * scale

    def sum_copy(way, k):
        return pltpu.make_async_remote_copy(
            src_ref=sum_out.at[way, k], dst_ref=sum_in.at[way, k],
            send_sem=s_send.at[way, k], recv_sem=s_recv.at[way, k],
            device_id=up if way == 0 else down, device_id_type=MESH)

    def sum_sends(k, way):
        return (nz - 1 - k > z) if way == 0 else (k < z)

    def sum_gets(k, way):
        return ((nz - 1 - k >= z) & has_down) if way == 0 else ((k <= z) & has_up)

    def sum_step(at):
        for way in range(2):
            k = at - z if way == 0 else at - (nz - 1 - z)
            j = nz - 1 - k if way == 0 else k

            @pl.when((k >= 0) & sum_gets(k, way))
            def _():
                sum_copy(way, k).wait_recv()

                @pl.when(j != z)
                def _():
                    sum_out[way, k] = (terms[j] + sum_in[way, k].astype(jnp.float32)).astype(jnp.bfloat16)

                @pl.when(j == z)
                def _():
                    terms[z] += sum_in[way, k].astype(jnp.float32)

            @pl.when((k >= 0) & sum_sends(k, way))
            def _():
                @pl.when(jnp.logical_not(sum_gets(k, way)))
                def _():
                    sum_out[way, k] = terms[j].astype(jnp.bfloat16)

                sum_copy(way, k).start()

    def z_pass(stream, c, h):
        for way in range(2):
            @pl.when(z_has(h, way))
            def _():
                z_wait_recv(stream, c, h, way)

                @pl.when(z_sends(h, way))
                def _():
                    z_copy(stream, c, h, way).start()

    z_start(0, 0, 0, True)
    for way in range(2):
        @pl.when(x_sends(0, way))
        def _():
            x_copy(0, way).start()
    twin_copy(0, 0).start()
    own_test.wait()

    @pl.loop(0, nz)
    def _(j):
        pltpu.make_async_copy(
            inv_ref.at[:, pl.ds(pl.multiple_of(j * fz, fz), fz)], inv.at[j], inv_sem.at[j]).wait()

    def term(j):
        terms[j] = jnp.dot(block(0, 1, z)[...], inv[j], preferred_element_type=jnp.float32)

    @pl.loop(0, nz)
    def _(k):
        term(jnp.where(k % 2 == 0, nz - 1 - k // 2, k // 2))

    sum_step(0)
    acc[...] = lax.dot_general(
        block(0, 0, z)[...], inv[z], LAST, preferred_element_type=jnp.float32)

    def precond(h):
        for way in range(2):
            @pl.when(z_has(h, way))
            def _():
                j = z - h if way == 0 else z + h
                acc[...] += lax.dot_general(
                    block(0, 0, j)[...], inv[j], LAST, preferred_element_type=jnp.float32)

    @pl.loop(1, nz - 1)
    def _(h):
        z_pass(0, 0, h)
        sum_step(h)
        precond(h)

    z_pass(0, 0, nz - 1)
    precond(nz - 1)
    block(1, 0, z)[...] = acc[...].astype(jnp.bfloat16)
    z_start(1, 0, 0)
    sum_step(nz - 1)
    block(1, 1, z)[...] = terms[z].astype(jnp.bfloat16)
    z_start(1, 1, 0)

    @pl.loop(1, nz - 1)
    def _(h):
        z_pass(1, 0, h)
        z_pass(1, 1, h)

    own_train.wait()
    for h in range(1, nx):
        for way in range(2):
            @pl.when(x_has(h, way))
            def _():
                x_wait_recv(h, way)

                @pl.when(x_sends(h, way))
                def _():
                    x_copy(h, way).start()

                twin_copy(h, way).start()
    twin_copy(0, 0, False).wait_recv()
    for h in range(1, nx):
        for way in range(2):
            @pl.when(x_has(h, way))
            def _():
                twin_copy(h, way, False).wait_recv()

    own = pl.ds(pl.multiple_of((z * fz) % fs, fz), fz)
    out_ref[...] = lax.dot_general(
        train_all[(z * fz) // fs, :, own], pre[:, pl.ds(pl.multiple_of(z * fz, fz), fz)], LAST,
        preferred_element_type=jnp.float32) * scale

    @pl.loop(1, nz - 1)
    def _(h):
        for way in range(2):
            @pl.when(z_has(h, way))
            def _():
                score(h, way)

    for c in range(chunks):
        z_pass(1, c, nz - 1)
        for way in range(2):
            @pl.when(z_has(nz - 1, way))
            def _():
                j = z - (nz - 1) if way == 0 else z + nz - 1
                cols = pl.ds(pl.multiple_of((j * fz) % fs, fz), fz)
                out_ref[:, c * part:(c + 1) * part] += lax.dot_general(
                    train_all[(j * fz) // fs, :, cols], block(1, c, j)[...], LAST,
                    preferred_element_type=jnp.float32) * scale

    twin_copy(0, 0).wait_send()
    for h in range(nx):
        for way in range(2):
            @pl.when(x_sends(h, way))
            def _():
                x_copy(h, way).wait_send()
            if h > 0:
                @pl.when(x_has(h, way))
                def _():
                    twin_copy(h, way).wait_send()

    @pl.loop(0, nz)
    def _(h):
        for way in range(2):
            for stream, c in ((0, 0), (1, 0), (1, 1)):
                @pl.when(z_sends(h, way))
                def _():
                    z_copy(stream, c, h, way).wait_send()

            @pl.when(sum_sends(h, way))
            def _():
                sum_copy(way, h).wait_send()


def shards(nz, nt, train_feat, test_feat, inverse_kernel):
    chunks = 2
    rows, fz = test_feat.shape
    train_rows, fs = train_feat.shape
    d = fz * nz
    nx = nt // CORES
    dma = pltpu.SemaphoreType.DMA
    anywhere = pl.BlockSpec(memory_space=pl.ANY)
    return pl.pallas_call(
        functools.partial(kernel, nz, nt, chunks),
        out_shape=jax.ShapeDtypeStruct((train_rows, rows), jnp.float32),
        in_specs=[anywhere] * 3,
        out_specs=pl.BlockSpec(memory_space=pltpu.VMEM),
        scratch_shapes=[
            pltpu.VMEM((rows, d), jnp.bfloat16),
            pltpu.VMEM((rows, d), jnp.bfloat16),
            pltpu.VMEM((nt, train_rows, fs), jnp.bfloat16),
            pltpu.VMEM((nz, fz, fz), jnp.bfloat16),
            pltpu.VMEM((rows // chunks, fz), jnp.float32),
            pltpu.VMEM((nz, rows // chunks, fz), jnp.float32),
            pltpu.VMEM((2, nz, rows // chunks, fz), jnp.bfloat16),
            pltpu.VMEM((2, nz, rows // chunks, fz), jnp.bfloat16),
            dma((2,)),
            dma((nz,)),
            dma((2, 2, chunks, nz)),
            dma((2, 2, chunks, nz)),
            dma((2, nx)),
            dma((2, nx)),
            dma((2, nx)),
            dma((2, nx)),
            dma((2, nz)),
            dma((2, nz)),
        ],
        compiler_params=pltpu.CompilerParams(
            collective_id=0, has_side_effects=True, vmem_limit_bytes=56 * 1024 * 1024),
        cost_estimate=pl.CostEstimate(
            flops=2 * rows * d * (fz + train_rows), bytes_accessed=16 * 2 ** 20, transcendentals=0),
    )(train_feat, test_feat, inverse_kernel)


def solution(mesh):
    placed = (P(("groups", "train"), "test"), P(("groups", "test"), "train"), P("train", None))
    return jax.shard_map(
        functools.partial(shards, mesh.shape["train"], mesh.shape["test"]),
        mesh=mesh,
        in_specs=placed,
        out_specs=P(("groups", "train"), "test"),
        check_vma=False,
    )
```

```python
import functools

import jax
import jax.numpy as jnp
from jax import lax
from jax.experimental import pallas as pl
from jax.experimental.pallas import tpu as pltpu
from jax.sharding import PartitionSpec as P

MESH = pl.DeviceIdType.MESH
CORES = 2
LAST = (((1,), (1,)), ((), ()))


def kernel(nz, nt, chunks, train_ref, test_ref, inv_ref, out_ref,
           feats, pre, train_all, inv, acc, terms, sum_in, sum_out,
           local_sem, inv_sem, z_send, z_recv, x_send, x_recv, c_send, c_recv, s_send, s_recv):
    nx = nt // CORES
    z = lax.axis_index("train")
    s = lax.axis_index("test")
    x, core = s // CORES, s % CORES
    twin = {"test": x * CORES + 1 - core}
    rows, fz = test_ref.shape
    fs = train_ref.shape[1]
    first = acc.shape[0]
    scale = 1.0 / (fz * nz) ** 0.5
    up, down = {"train": z + 1}, {"train": z - 1}
    has_up, has_down = z < nz - 1, z > 0

    def as_int(flag):
        return jnp.where(flag, 1, 0)

    barrier = pltpu.get_barrier_semaphore()
    pl.semaphore_signal(barrier, inc=1, device_id=twin, device_id_type=MESH)
    links = 1 + as_int(has_up) + as_int(has_down) + as_int(x > 0) + as_int(x < nx - 1)

    @pl.when(has_up)
    def _():
        pl.semaphore_signal(barrier, inc=1, device_id=up, device_id_type=MESH)

    @pl.when(has_down)
    def _():
        pl.semaphore_signal(barrier, inc=1, device_id=down, device_id_type=MESH)

    @pl.when(x > 0)
    def _():
        pl.semaphore_signal(barrier, inc=1, device_id={"test": s - CORES}, device_id_type=MESH)

    @pl.when(x < nx - 1)
    def _():
        pl.semaphore_signal(barrier, inc=1, device_id={"test": s + CORES}, device_id_type=MESH)

    own_test = pltpu.make_async_copy(
        test_ref, feats.at[:, pl.ds(pl.multiple_of(z * fz, fz), fz)], local_sem.at[0])
    own_train = pltpu.make_async_copy(train_ref, train_all.at[s], local_sem.at[1])
    own_test.start()

    @pl.loop(0, nz)
    def _(j):
        pltpu.make_async_copy(
            inv_ref.at[:, pl.ds(pl.multiple_of(j * fz, fz), fz)], inv.at[j], inv_sem.at[j]).start()

    own_train.start()
    pl.semaphore_wait(barrier, links)

    def block(stream, c, j):
        buf = (feats, pre)[stream]
        at = pl.ds(0, first) if c == 0 else pl.ds(first, rows - first)
        return buf.at[at, pl.ds(pl.multiple_of(j * fz, fz), fz)]

    def z_copy(stream, c, h, way, fresh=False):
        j = z - h if way == 0 else z + h
        dst = block(stream, c, j)
        src = test_ref.at[pl.ds(0, first), :] if fresh and stream == 0 else dst
        return pltpu.make_async_remote_copy(
            src_ref=src, dst_ref=dst,
            send_sem=z_send.at[stream, way, c, h], recv_sem=z_recv.at[stream, way, c, h],
            device_id=up if way == 0 else down, device_id_type=MESH)

    def z_sends(h, way):
        return ((z >= h) & has_up) if way == 0 else ((z + h < nz) & has_down)

    def z_start(stream, c, h, fresh=False):
        for way in range(2):
            @pl.when(z_sends(h, way))
            def _():
                z_copy(stream, c, h, way, fresh).start()

    def z_wait_recv(stream, c, h, way):
        j = z - h if way == 0 else z + h
        dst = block(stream, c, j)
        pltpu.make_async_remote_copy(
            src_ref=dst, dst_ref=dst,
            send_sem=z_send.at[stream, way, c, h - 1], recv_sem=z_recv.at[stream, way, c, h - 1],
            device_id=down if way == 0 else up, device_id_type=MESH).wait_recv()

    def z_has(h, way):
        return (z >= h) if way == 0 else (z + h < nz)

    def x_copy(h, way):
        owner = s - CORES * h if way == 0 else s + CORES * h
        return pltpu.make_async_remote_copy(
            src_ref=train_ref if h == 0 else train_all.at[owner], dst_ref=train_all.at[owner],
            send_sem=x_send.at[way, h], recv_sem=x_recv.at[way, h],
            device_id={"test": s + CORES if way == 0 else s - CORES}, device_id_type=MESH)

    def x_has(h, way):
        return (x >= h) if way == 0 else (x + h < nx)

    def x_sends(h, way):
        return x_has(h, way) & ((x < nx - 1) if way == 0 else (x > 0))

    def x_wait_recv(h, way):
        owner = s - CORES * h if way == 0 else s + CORES * h
        pltpu.make_async_remote_copy(
            src_ref=train_all.at[owner], dst_ref=train_all.at[owner],
            send_sem=x_send.at[way, h - 1], recv_sem=x_recv.at[way, h - 1],
            device_id={"test": s - CORES if way == 0 else s + CORES}, device_id_type=MESH).wait_recv()

    def twin_copy(h, way, mine=True):
        c = core if mine else 1 - core
        owner = (x - h if way == 0 else x + h) * CORES + c
        return pltpu.make_async_remote_copy(
            src_ref=train_ref if h == 0 else train_all.at[owner], dst_ref=train_all.at[owner],
            send_sem=c_send.at[way, h], recv_sem=c_recv.at[way, h],
            device_id=twin, device_id_type=MESH)

    def score(h, way):
        j = z - h if way == 0 else z + h
        at = j * fz
        cols = pl.ds(pl.multiple_of(at % fs, fz), fz)
        out_ref[...] += lax.dot_general(
            train_all[at // fs, :, cols], pre[:, pl.ds(pl.multiple_of(at, fz), fz)], LAST,
            preferred_element_type=jnp.float32) * scale

    def sum_copy(way, k):
        return pltpu.make_async_remote_copy(
            src_ref=sum_out.at[way, k], dst_ref=sum_in.at[way, k],
            send_sem=s_send.at[way, k], recv_sem=s_recv.at[way, k],
            device_id=up if way == 0 else down, device_id_type=MESH)

    def sum_sends(k, way):
        return (nz - 1 - k > z) if way == 0 else (k < z)

    def sum_gets(k, way):
        return ((nz - 1 - k >= z) & has_down) if way == 0 else ((k <= z) & has_up)

    def sum_step(at):
        for way in range(2):
            k = at - z if way == 0 else at - (nz - 1 - z)
            j = nz - 1 - k if way == 0 else k

            @pl.when((k >= 0) & sum_gets(k, way))
            def _():
                sum_copy(way, k).wait_recv()

                @pl.when(j != z)
                def _():
                    sum_out[way, k] = (terms[j] + sum_in[way, k].astype(jnp.float32)).astype(jnp.bfloat16)

                @pl.when(j == z)
                def _():
                    terms[z] += sum_in[way, k].astype(jnp.float32)

            @pl.when((k >= 0) & sum_sends(k, way) & (has_down if way == 0 else has_up))
            def _():
                sum_copy(way, k).start()

    def sum_source(k):
        for way in range(2):
            j = nz - 1 - k if way == 0 else k

            @pl.when(jnp.logical_not(has_down if way == 0 else has_up) & (k < nz - 1))
            def _():
                sum_out[way, k] = terms[j].astype(jnp.bfloat16)
                sum_copy(way, k).start()

    def z_pass(stream, c, h):
        for way in range(2):
            @pl.when(z_has(h, way))
            def _():
                z_wait_recv(stream, c, h, way)

                @pl.when(z_sends(h, way))
                def _():
                    z_copy(stream, c, h, way).start()

    z_start(0, 0, 0, True)
    for way in range(2):
        @pl.when(x_sends(0, way))
        def _():
            x_copy(0, way).start()
    twin_copy(0, 0).start()
    own_test.wait()

    @pl.loop(0, nz)
    def _(j):
        pltpu.make_async_copy(
            inv_ref.at[:, pl.ds(pl.multiple_of(j * fz, fz), fz)], inv.at[j], inv_sem.at[j]).wait()

    def term(j):
        terms[j] = jnp.dot(block(0, 1, z)[...], inv[j], preferred_element_type=jnp.float32)

    @pl.loop(0, nz)
    def _(k):
        term(jnp.where(k % 2 == 0, nz - 1 - k // 2, k // 2))

    ahead = 1
    for k in range(min(ahead + 1, nz - 1)):
        sum_source(k)
    acc[...] = lax.dot_general(
        block(0, 0, z)[...], inv[z], LAST, preferred_element_type=jnp.float32)

    def precond(h):
        for way in range(2):
            @pl.when(z_has(h, way))
            def _():
                j = z - h if way == 0 else z + h
                acc[...] += lax.dot_general(
                    block(0, 0, j)[...], inv[j], LAST, preferred_element_type=jnp.float32)

    def gather_first():
        block(1, 0, z)[...] = acc[...].astype(jnp.bfloat16)
        z_start(1, 0, 0)

    @pl.loop(1, nz - 1)
    def _(h):
        z_pass(0, 0, h)
        sum_source(h + ahead)

        @pl.when(h < nz - 2)
        def _():
            sum_step(h)

        precond(h)

    inside = has_up & has_down

    @pl.when(inside)
    def _():
        gather_first()

    if nz > 2:
        sum_step(nz - 2)
    z_pass(0, 0, nz - 1)

    @pl.when(jnp.logical_not(inside))
    def _():
        precond(nz - 1)
        gather_first()

    sum_step(nz - 1)
    block(1, 1, z)[...] = terms[z].astype(jnp.bfloat16)
    z_start(1, 1, 0)

    @pl.loop(1, nz - 1)
    def _(h):
        z_pass(1, 0, h)
        z_pass(1, 1, h)

    own_train.wait()
    for h in range(1, nx):
        for way in range(2):
            @pl.when(x_has(h, way))
            def _():
                x_wait_recv(h, way)

                @pl.when(x_sends(h, way))
                def _():
                    x_copy(h, way).start()

                twin_copy(h, way).start()
    twin_copy(0, 0, False).wait_recv()
    for h in range(1, nx):
        for way in range(2):
            @pl.when(x_has(h, way))
            def _():
                twin_copy(h, way, False).wait_recv()

    out_ref[...] = jnp.zeros(out_ref.shape, jnp.float32)
    score(0, 0)

    @pl.loop(1, nz - 1)
    def _(h):
        for way in range(2):
            @pl.when(z_has(h, way))
            def _():
                score(h, way)

    z_pass(1, 0, nz - 1)
    z_pass(1, 1, nz - 1)
    for way in range(2):
        @pl.when(z_has(nz - 1, way))
        def _():
            score(nz - 1, way)

    twin_copy(0, 0).wait_send()
    for h in range(nx):
        for way in range(2):
            @pl.when(x_sends(h, way))
            def _():
                x_copy(h, way).wait_send()
            if h > 0:
                @pl.when(x_has(h, way))
                def _():
                    twin_copy(h, way).wait_send()

    @pl.loop(0, nz)
    def _(h):
        for way in range(2):
            for stream, c in ((0, 0), (1, 0), (1, 1)):
                @pl.when(z_sends(h, way))
                def _():
                    z_copy(stream, c, h, way).wait_send()

            @pl.when(sum_sends(h, way))
            def _():
                sum_copy(way, h).wait_send()


def shards(nz, nt, train_feat, test_feat, inverse_kernel):
    chunks = 2
    rows, fz = test_feat.shape
    first = rows * 8 // 16 // 16 * 16
    train_rows, fs = train_feat.shape
    d = fz * nz
    nx = nt // CORES
    dma = pltpu.SemaphoreType.DMA
    anywhere = pl.BlockSpec(memory_space=pl.ANY)
    return pl.pallas_call(
        functools.partial(kernel, nz, nt, chunks),
        out_shape=jax.ShapeDtypeStruct((train_rows, rows), jnp.float32),
        in_specs=[anywhere] * 3,
        out_specs=pl.BlockSpec(memory_space=pltpu.VMEM),
        scratch_shapes=[
            pltpu.VMEM((rows, d), jnp.bfloat16),
            pltpu.VMEM((rows, d), jnp.bfloat16),
            pltpu.VMEM((nt, train_rows, fs), jnp.bfloat16),
            pltpu.VMEM((nz, fz, fz), jnp.bfloat16),
            pltpu.VMEM((first, fz), jnp.float32),
            pltpu.VMEM((nz, rows - first, fz), jnp.float32),
            pltpu.VMEM((2, nz, rows - first, fz), jnp.bfloat16),
            pltpu.VMEM((2, nz, rows - first, fz), jnp.bfloat16),
            dma((2,)),
            dma((nz,)),
            dma((2, 2, chunks, nz)),
            dma((2, 2, chunks, nz)),
            dma((2, nx)),
            dma((2, nx)),
            dma((2, nx)),
            dma((2, nx)),
            dma((2, nz)),
            dma((2, nz)),
        ],
        compiler_params=pltpu.CompilerParams(
            collective_id=0, has_side_effects=True, vmem_limit_bytes=56 * 1024 * 1024),
        cost_estimate=pl.CostEstimate(
            flops=2 * rows * d * (fz + train_rows), bytes_accessed=16 * 2 ** 20, transcendentals=0),
    )(train_feat, test_feat, inverse_kernel)


def solution(mesh):
    placed = (P(("groups", "train"), "test"), P(("groups", "test"), "train"), P("train", None))
    return jax.shard_map(
        functools.partial(shards, mesh.shape["train"], mesh.shape["test"]),
        mesh=mesh,
        in_specs=placed,
        out_specs=P(("groups", "train"), "test"),
        check_vma=False,
    )
```
